32 devices in a mesh: req: 16 (over z, y, x), hist: 2 (over core).
Axes of the slice: x: 2, y: 2, z: 4, core: 2. Of those that a mesh axis runs over, the one named last changes fastest.
Arguments:
- cand_embed: bfloat16 [16, 768, 1024], P('req', 'hist'), may hold values from -6 to 6
- hist_keys: bfloat16 [16, 256, 1024], P('req', 'hist'), may hold values from -6 to 6
- hist_values: bfloat16 [16, 256, 1024], P('req', 'hist'), may hold values from -6 to 6
- in_weight: bfloat16 [1024, 4096], P('req'), may hold values from -0.1875 to 0.1875
- out_weight: bfloat16 [1024, 1024], replicated, may hold values from -0.1875 to 0.1875
- norm_gain: float32 [1024], replicated, may hold values from 0.25 to 1.75
- cand_counts: int32 [16], P('req'), may hold values from 96 to 768, as said below
- hist_lengths: int32 [16], P('req'), may hold values from 128 to 256, as said below
- self_mask: int32 [16, 768, 64], P('req', 'hist'), may hold values 0 or 1
Outputs:
- cand_out: bfloat16 [16, 768, 1024], P('req', 'hist')
The draws below stay inside these ranges and needn't reach their ends.
Inputs may be any that keep to these rules, and one draw needn't show every extreme that they name: `cand_counts`: in every draw one request has all 768 candidate slots live; the others have between 96 and 256. `hist_lengths`: multiples of 128; in every draw one request has the full 256.
All inputs are finite; a program needn't handle non-finite values. No bound on the sum of `self_mask` on one device may be relied on, other than what follows from the above.
Results may differ from the reference program's by a relative error of at most 0.0027.
Values may be sent and summed in bfloat16 or wider, within the bound.
A program may use at most 128 MiB of HBM per device.

```python
import jax
import jax.numpy as jnp
from jax import lax

D = 1024
HEADS = 8
SELF_BLOCK = 64
REQUESTS = 16
CANDS = 768
HIST = 256


def draw_cand_counts(key, part):
    counts = jax.random.randint(key, (REQUESTS,), CANDS // 8, CANDS // 3 + 1)
    chosen = jax.random.randint(jax.random.fold_in(key, 7), (), 0, REQUESTS)
    return jnp.where(jnp.arange(REQUESTS) == chosen, CANDS, counts).astype(jnp.int32)


def draw_hist_lengths(key, part):
    units = jax.random.randint(key, (REQUESTS,), 1, HIST // 128 + 1)
    chosen = jax.random.randint(jax.random.fold_in(key, 11), (), 0, REQUESTS)
    units = jnp.where(jnp.arange(REQUESTS) == chosen, HIST // 128, units)
    return (units * 128).astype(jnp.int32)


def with_ends(drawn, key, smallest, high):
    shape = drawn.shape
    place = [jax.random.randint(jax.random.fold_in(key, axis), (), 0, shape[axis]) for axis in range(len(shape))]
    drawn = drawn.at[tuple(place)].set(smallest)
    longest = shape.index(max(shape))
    place[longest] = (place[longest] + 1) % shape[longest]
    return drawn.at[tuple(place)].set(high)


def block_scale(stream_key, shape, shards, smallest, largest):
    def one(axis_at, blocks):
        draws = jax.random.uniform(jax.random.fold_in(jax.random.fold_in(stream_key, 6), axis_at), (blocks,), jnp.float32, smallest / len(shards), largest / len(shards))
        return jnp.repeat(jnp.exp(draws), shape[axis_at] // blocks).reshape((-1,) + (1,) * (len(shape) - axis_at - 1))

    level = one(*shards[0])
    for cut in shards[1:]:
        level = level * one(*cut)
    return level


def gaussian(own_key, dims, spread, reach, shards=(), kind=jnp.bfloat16):
    values = jax.random.normal(own_key, dims, jnp.float32) * spread
    if len(shards) > 0:
        values = block_scale(own_key, dims, shards, -0.22, 0.18) * values
    return jnp.clip(values, min=-reach, max=reach).astype(kind)


def setup_inputs(seed: int = 0) -> dict:
    splits = jax.random.split(jax.random.key(seed), 10)
    return {
        "cand_embed": gaussian(splits[0], (REQUESTS, CANDS, D), 1.0, 6.0, ((0, 16), (1, 2))),
        "hist_keys": gaussian(splits[1], (REQUESTS, HIST, D), 1.0, 6.0, ((0, 16), (1, 2))),
        "hist_values": gaussian(splits[2], (REQUESTS, HIST, D), 1.0, 6.0, ((0, 16), (1, 2))),
        "in_weight": gaussian(splits[3], (D, 4 * D), D ** -0.5, 0.1875, ((0, 16),)),
        "out_weight": gaussian(splits[4], (D, D), D ** -0.5, 0.1875),
        "norm_gain": jnp.clip(1.0 + 0.15 * jax.random.normal(splits[5], (D,), jnp.float32), 0.25, 1.75),
        "cand_counts": draw_cand_counts(jax.random.fold_in(splits[9], 71), 0),
        "hist_lengths": draw_hist_lengths(jax.random.fold_in(splits[9], 71), 0),
        "self_mask": with_ends((jax.random.randint(splits[8], (REQUESTS, CANDS, SELF_BLOCK), 0, 2) < 1).astype(jnp.int32), jax.random.fold_in(splits[8], 1), 0, 1),
    }


def one_request(cand_row, keys_row, values_row, count, length, mask_row, in_weight, out_weight, norm_gain):
    head_dim = D // HEADS
    scale_factor = head_dim ** (-0.5)
    projected = jax.nn.silu(jnp.dot(cand_row, in_weight, preferred_element_type=jnp.float32)).astype(jnp.bfloat16)
    gate_u = projected[:, :D]
    self_values = projected[:, D:2 * D]
    queries = projected[:, 2 * D:3 * D]
    self_keys = projected[:, 3 * D:]
    is_live = jnp.arange(CANDS) < count
    divisor = (length + SELF_BLOCK).astype(jnp.float32)
    query_heads = queries.astype(jnp.float32).reshape(CANDS, HEADS, head_dim)
    key_heads = keys_row.astype(jnp.float32).reshape(HIST, HEADS, head_dim)
    value_heads = values_row.astype(jnp.float32).reshape(HIST, HEADS, head_dim)
    scores = jnp.einsum('chd,nhd->hcn', query_heads, key_heads) * scale_factor
    visible = (jnp.arange(HIST) < length).astype(jnp.float32)
    hist_mix = (jax.nn.silu(scores) * visible[None, None, :] / divisor).astype(jnp.bfloat16)
    attended = jnp.einsum('hcn,nhd->chd', hist_mix.astype(jnp.float32), value_heads)
    blocks = CANDS // SELF_BLOCK
    query_blocks = query_heads.reshape(blocks, SELF_BLOCK, HEADS, head_dim)
    key_blocks = self_keys.astype(jnp.float32).reshape(blocks, SELF_BLOCK, HEADS, head_dim)
    value_blocks = self_values.astype(jnp.float32).reshape(blocks, SELF_BLOCK, HEADS, head_dim)
    self_scores = jnp.einsum('bphd,bchd->bhpc', query_blocks, key_blocks) * scale_factor
    position = jnp.arange(SELF_BLOCK)
    causal = position[None, :] <= position[:, None]
    diagonal = position[None, :] == position[:, None]
    given = mask_row.reshape(blocks, SELF_BLOCK, SELF_BLOCK) == 1
    key_live = is_live.reshape(blocks, 1, SELF_BLOCK)
    allowed = (causal[None] & (given | diagonal[None]) & key_live).astype(jnp.float32)
    self_mix = (jax.nn.silu(self_scores) * allowed[:, None, :, :] / divisor).astype(jnp.bfloat16)
    self_part = jnp.einsum('bhpc,bchd->bphd', self_mix.astype(jnp.float32), value_blocks)
    attended = (attended + self_part.reshape(CANDS, HEADS, head_dim)).reshape(CANDS, D)
    average = lax.optimization_barrier(jnp.mean(attended, axis=1, keepdims=True))
    variance = lax.optimization_barrier(jnp.mean((attended - average) ** 2, axis=1, keepdims=True))
    gated = ((attended - average) / jnp.sqrt(variance + 1e-05) * norm_gain * gate_u.astype(jnp.float32)).astype(jnp.bfloat16)
    branch = jnp.dot(gated, out_weight, preferred_element_type=jnp.float32)
    result = cand_row.astype(jnp.float32) + is_live.astype(jnp.float32)[:, None] * branch
    return result.astype(jnp.bfloat16)

def reference(cand_embed, hist_keys, hist_values, in_weight, out_weight, norm_gain, cand_counts, hist_lengths, self_mask):

    def step(packed):
        cand_row, keys_row, values_row, count, length, mask_row = packed
        return one_request(cand_row, keys_row, values_row, count, length, mask_row, in_weight, out_weight, norm_gain)
    return lax.map(step, (cand_embed, hist_keys, hist_values, cand_counts, hist_lengths, self_mask))
```

```python
import functools

import jax
import jax.numpy as jnp
from jax import lax
from jax.experimental import pallas as pl
from jax.experimental.pallas import tpu as pltpu
from jax.sharding import PartitionSpec as P

HEADS = 8
SELF_BLOCK = 64
MESH = pl.DeviceIdType.MESH
LINE = 4
PLANE = 4
GROUPS = (2, 3, 1, 0)


def interleave(events, work, start):
    slots = max(len(events) - start, 1)
    done = 0
    for at, event in enumerate(events):
        event()
        if at >= start:
            upto = (at - start + 1) * len(work) // slots
            for job in work[done:upto]:
                job()
            done = max(done, upto)
    for job in work[done:]:
        job()


def silu(x):
    half = x * 0.5
    return half + half * jnp.tanh(half)


def layer_kernel(
    cand_hbm, hk_hbm, hv_hbm, w_ref, wout_hbm, gain_ref, count_ref, length_ref, mask_ref,
    out_ref,
    cand, hist_k, hist_v, wbuf, wout, mask, amask, q, k, v, att, st_mine, st_other,
    g_mine, g_send, g_recv,
    send_x, send_y, send_up, send_down, recv, sib_send, sib_recv, local_sem,
):
    rows, width = cand_hbm.shape
    all_rows = 2 * rows
    depth = w_ref.shape[0]
    half = width // 2
    hist_rows = hk_hbm.shape[0]
    span = 2 * hist_rows
    heads = HEADS // 2
    head_dim = width // HEADS
    scale = head_dim ** (-0.5)

    me = lax.axis_index("req")
    core = lax.axis_index("hist")
    other = 1 - core
    z = me // PLANE
    plane = me - z * PLANE
    y = plane // 2
    x = plane - 2 * y
    plane_x = 2 * y + (1 - x)
    plane_y = 2 * (1 - y) + x
    plane_d = 2 * (1 - y) + (1 - x)
    to_x = {"req": z * PLANE + plane_x}
    to_y = {"req": z * PLANE + plane_y}
    to_up = {"req": me + PLANE}
    to_down = {"req": me - PLANE}
    sibling = {"hist": other}
    has_up = z < LINE - 1
    has_down = z > 0
    near = z + 1 - 2 * (z // 3)
    far = 3 * (1 - z // 2)
    near_z = (z, near, 6 - z - near - far, far)

    my_cols = pl.ds(pl.multiple_of(core * half, half), half)
    other_cols = pl.ds(pl.multiple_of(other * half, half), half)
    my_rows = pl.ds(pl.multiple_of(core * rows, rows), rows)
    other_rows = pl.ds(pl.multiple_of(other * rows, rows), rows)
    my_hist = pl.ds(pl.multiple_of(core * hist_rows, hist_rows), hist_rows)
    locals_ = [
        pltpu.make_async_copy(cand_hbm, cand.at[my_rows], local_sem.at[0]),
        pltpu.make_async_copy(hk_hbm.at[:, my_cols], hist_k.at[my_hist], local_sem.at[1]),
        pltpu.make_async_copy(hv_hbm.at[:, my_cols], hist_v.at[my_hist], local_sem.at[2]),
        pltpu.make_async_copy(mask_ref, mask.at[my_rows], local_sem.at[3]),
        pltpu.make_async_copy(wout_hbm, wout, local_sem.at[4]),
    ]
    for copy in locals_:
        copy.start()

    barrier = pltpu.get_barrier_semaphore()

    def greet(target):
        pl.semaphore_signal(barrier, inc=1, device_id=target, device_id_type=MESH)

    greet(to_x)
    greet(to_y)
    greet(sibling)
    pl.when(has_up)(lambda: greet(to_up))
    pl.when(has_down)(lambda: greet(to_down))
    pl.semaphore_wait(barrier, 3 + (1 - z // (LINE - 1)) + (z + LINE - 2) // (LINE - 1))

    def slot(g, chip):
        return wbuf.at[g, pl.ds(pl.multiple_of(chip * depth, depth), depth)]

    def remote(src, dst, ssem, rsem, target):
        return pltpu.make_async_remote_copy(
            src_ref=src, dst_ref=dst, send_sem=ssem, recv_sem=rsem,
            device_id=target, device_id_type=MESH,
        )

    def own_piece(g):
        start = pl.multiple_of(GROUPS[g] * width + core * half, half)
        return w_ref.at[:, pl.ds(start, half)]

    def send(g, chip, sem, target, src=None):
        here = slot(g, chip) if src is None else src
        remote(here, slot(g, chip), sem, recv.at[g, chip], target).start()

    def arrived(g, chip):
        remote(slot(g, chip), slot(g, chip), recv.at[g, chip], recv.at[g, chip], to_x).wait_recv()

    def own(g):
        src = own_piece(g)
        send(g, me, send_x.at[g, z], to_x, src)
        send(g, me, send_y.at[g, z], to_y, src)
        pl.when(has_up)(lambda: send(g, me, send_up.at[g, z], to_up, src))
        pl.when(has_down)(lambda: send(g, me, send_down.at[g, z], to_down, src))

    def from_line(g, offset):
        at = z + offset
        chip = me + offset * PLANE

        def body():
            arrived(g, chip)
            if offset < 0:
                pl.when(has_up)(lambda: send(g, chip, send_up.at[g, at], to_up))
            else:
                pl.when(has_down)(lambda: send(g, chip, send_down.at[g, at], to_down))
            send(g, chip, send_x.at[g, at], to_x)
            send(g, chip, send_y.at[g, at], to_y)

        pl.when((at >= 0) if offset < 0 else (at < LINE))(body)

    def from_sides(g, step):
        at = near_z[step]
        even = at % 2 == 0
        chip_x = at * PLANE + plane_x
        chip_y = at * PLANE + plane_y
        arrived(g, chip_x)
        pl.when(even)(lambda: send(g, chip_x, send_y.at[g, LINE + at], to_y))
        arrived(g, chip_y)
        pl.when(jnp.logical_not(even))(
            lambda: send(g, chip_y, send_x.at[g, LINE + at], to_x)
        )

    def from_diagonal(g):
        for at in near_z:
            arrived(g, at * PLANE + plane_d)

    def forwards(g):
        part = functools.partial
        events = [part(from_line, g, -1), part(from_line, g, 1), part(from_sides, g, 0)]
        events += [part(from_line, g, -2), part(from_line, g, 2)]
        events += [part(from_sides, g, 1), part(from_sides, g, 2)]
        events += [part(from_line, g, -3), part(from_line, g, 3)]
        if g + 1 < len(GROUPS):
            events += [part(own, g + 1)]
        events += [part(from_sides, g, 3)]
        return events

    own(0)

    sib = [
        remote(cand_hbm, cand.at[my_rows], sib_send.at[0], sib_recv.at[0], sibling),
        remote(hk_hbm.at[:, other_cols], hist_k.at[my_hist], sib_send.at[1], sib_recv.at[1], sibling),
        remote(hv_hbm.at[:, other_cols], hist_v.at[my_hist], sib_send.at[2], sib_recv.at[2], sibling),
        remote(mask_ref, mask.at[my_rows], sib_send.at[3], sib_recv.at[3], sibling),
    ]
    for copy in sib:
        copy.start()

    for g in range(len(GROUPS)):
        wbuf[g, pl.ds(pl.multiple_of(me * depth, depth), depth), :] = own_piece(g)[...]

    count = count_ref[0]
    length = length_ref[0]
    divisor = (length + SELF_BLOCK).astype(jnp.float32)

    def inputs_here():
        for copy in locals_:
            copy.wait()
        for copy in sib:
            copy.wait_recv()

    tile = 2 * SELF_BLOCK
    tiles = all_rows // tile

    def make_mask(t):
        r0 = t * tile
        row = lax.broadcasted_iota(jnp.int32, (tile, tile), 0)
        col = lax.broadcasted_iota(jnp.int32, (tile, tile), 1)
        given = mask[pl.ds(r0, tile), :]
        given = jnp.concatenate([given, given], axis=1)
        keep = (
            (row // SELF_BLOCK == col // SELF_BLOCK)
            & (col <= row)
            & ((given == 1) | (row == col))
            & (r0 + col < count)
        )
        amask[pl.ds(r0, tile), :] = jnp.where(keep, 1.0 / divisor, 0.0)

    def masks():
        for t in range(tiles):
            make_mask(t)

    cols = half // 2

    def project(g, dst, r, n):
        acc = jnp.dot(
            cand[pl.ds(r * rows, rows), :],
            wbuf[g, :, pl.ds(n * cols, cols)],
            preferred_element_type=jnp.float32,
        )
        dst[pl.ds(r * rows, rows), pl.ds(n * cols, cols)] = silu(acc).astype(jnp.bfloat16)

    def projections(g, dst):
        return [functools.partial(project, g, dst, r, n) for n in range(2) for r in range(2)]

    nt = (((1,), (1,)), ((), ()))

    def hist_part(t):
        r0 = t * tile
        col = lax.broadcasted_iota(jnp.int32, (1, span), 1)
        weight = jnp.where(col < length, 1.0 / divisor, 0.0)
        for h in range(heads):
            hc = slice(h * head_dim, (h + 1) * head_dim)
            s = lax.dot_general(
                q[pl.ds(r0, tile), hc], hist_k[:, hc], nt, preferred_element_type=jnp.float32
            )
            mix = (silu(s * scale) * weight).astype(jnp.bfloat16)
            att[pl.ds(r0, tile), hc] = jnp.dot(
                mix, hist_v[:, hc], preferred_element_type=jnp.float32
            )

    def self_part(t):
        r0 = t * tile
        for h in range(heads):
            hc = slice(h * head_dim, (h + 1) * head_dim)
            s = lax.dot_general(
                q[pl.ds(r0, tile), hc], k[pl.ds(r0, tile), hc], nt,
                preferred_element_type=jnp.float32,
            )
            mix = (silu(s * scale) * amask[pl.ds(r0, tile), :]).astype(jnp.bfloat16)
            att[pl.ds(r0, tile), hc] += jnp.dot(
                mix, v[pl.ds(r0, tile), hc], preferred_element_type=jnp.float32
            )
        here = att[pl.ds(r0, tile), :]
        mean = jnp.mean(here, axis=1, keepdims=True)
        spread = jnp.sum((here - mean) ** 2, axis=1, keepdims=True)
        lane = lax.broadcasted_iota(jnp.int32, (tile, 128), 1)
        st_mine[pl.ds(r0, tile), :] = jnp.where(lane < 64, mean, spread)

    stats = remote(st_mine, st_other, sib_send.at[4], sib_recv.at[4], sibling)

    def normalise(t):
        r0 = t * tile
        mine, theirs = st_mine[pl.ds(r0, tile), :], st_other[pl.ds(r0, tile), :]
        mean_a, mean_b = mine[:, 0:1], theirs[:, 0:1]
        gap = mean_a - mean_b
        mean = 0.5 * (mean_a + mean_b)
        variance = (mine[:, 64:65] + theirs[:, 64:65] + gap * gap * (half / 2)) / width
        factor = lax.rsqrt(variance + 1e-05)
        att[pl.ds(r0, tile), :] = (
            (att[pl.ds(r0, tile), :] - mean) * factor * gain_ref[:, my_cols]
        )

    part = functools.partial
    interleave(forwards(0), [], 0)
    inputs_here()
    masks()
    interleave(
        forwards(1)[:4] + [part(from_diagonal, 0)] + forwards(1)[4:], projections(0, q), 4
    )
    work = projections(1, k) + [part(hist_part, t) for t in range(tiles)]
    interleave(forwards(2)[:4] + [part(from_diagonal, 1)] + forwards(2)[4:], work, 4)
    work = projections(2, v) + [part(self_part, t) for t in range(tiles)]
    work += [stats.start]
    interleave(forwards(3)[:4] + [part(from_diagonal, 2)] + forwards(3)[4:], work, 4)
    stats.wait_recv()
    for t in range(tiles):
        normalise(t)

    def gate(dst, at):
        for n in range(2):
            nc = pl.ds(n * cols, cols)
            acc = jnp.dot(
                cand[at, :], wbuf[3, :, nc], preferred_element_type=jnp.float32
            )
            u = silu(acc).astype(jnp.bfloat16).astype(jnp.float32)
            dst[:, nc] = (att[at, nc] * u).astype(jnp.bfloat16)

    from_diagonal(3)
    gate(g_send, other_rows)
    gated = remote(g_send, g_recv, sib_send.at[5], sib_recv.at[5], sibling)
    gated.start()
    gate(g_mine, my_rows)
    live_row = core * rows + lax.broadcasted_iota(jnp.int32, (rows, 1), 0)
    live = jnp.where(live_row < count, 1.0, 0.0)
    for n in range(4):
        nc = slice(n * 256, (n + 1) * 256)
        att_cols = pl.ds((n % 2) * 256, 256)
        att[pl.ds((n // 2) * rows, rows), att_cols] = jnp.dot(
            g_mine[...], wout[my_cols, nc], preferred_element_type=jnp.float32
        )
    gated.wait_recv()
    for n in range(4):
        nc = slice(n * 256, (n + 1) * 256)
        att_cols = pl.ds((n % 2) * 256, 256)
        branch = att[pl.ds((n // 2) * rows, rows), att_cols] + jnp.dot(
            g_recv[...], wout[other_cols, nc], preferred_element_type=jnp.float32
        )
        res = cand[my_rows, nc].astype(jnp.float32) + live * branch
        out_ref[:, nc] = res.astype(jnp.bfloat16)

    for copy in sib:
        copy.wait_send()
    stats.wait_send()
    gated.wait_send()

    def left(sem):
        piece = slot(0, 0)
        remote(piece, piece, sem, sem, to_x).wait_send()

    for g in range(len(GROUPS)):
        for at in range(LINE):
            left(send_x.at[g, at])
            left(send_y.at[g, at])
            if at % 2 == 0:
                left(send_y.at[g, LINE + at])
            else:
                left(send_x.at[g, LINE + at])
            pl.when(has_up & (at <= z))(lambda: left(send_up.at[g, at]))
            pl.when(has_down & (at >= z))(lambda: left(send_down.at[g, at]))


def on_device_kernel(
    cand_embed, hist_keys, hist_values, in_weight, out_weight, norm_gain,
    cand_counts, hist_lengths, self_mask,
):
    _, rows, width = cand_embed.shape
    hist_rows = hist_keys.shape[1]
    half = width // 2
    depth = in_weight.shape[0]
    bf16, f32 = jnp.bfloat16, jnp.float32
    groups = len(GROUPS)
    vmem = pl.BlockSpec(memory_space=pltpu.VMEM)
    smem = pl.BlockSpec(memory_space=pltpu.SMEM)
    hbm = pl.BlockSpec(memory_space=pl.ANY)
    dma = pltpu.SemaphoreType.DMA
    out = pl.pallas_call(
        layer_kernel,
        out_shape=jax.ShapeDtypeStruct((rows, width), bf16),
        in_specs=[hbm, hbm, hbm, vmem, hbm, vmem, smem, smem, vmem],
        out_specs=vmem,
        scratch_shapes=[
            pltpu.VMEM((2 * rows, width), bf16),
            pltpu.VMEM((2 * hist_rows, half), bf16),
            pltpu.VMEM((2 * hist_rows, half), bf16),
            pltpu.VMEM((groups, width, half), bf16),
            pltpu.VMEM((width, width), bf16),
            pltpu.VMEM((2 * rows, SELF_BLOCK), jnp.int32),
            pltpu.VMEM((2 * rows, 2 * SELF_BLOCK), f32),
            pltpu.VMEM((2 * rows, half), bf16),
            pltpu.VMEM((2 * rows, half), bf16),
            pltpu.VMEM((2 * rows, half), bf16),
            pltpu.VMEM((2 * rows, half), f32),
            pltpu.VMEM((2 * rows, 128), f32),
            pltpu.VMEM((2 * rows, 128), f32),
            pltpu.VMEM((rows, half), bf16),
            pltpu.VMEM((rows, half), bf16),
            pltpu.VMEM((rows, half), bf16),
            dma((groups, 2 * LINE)),
            dma((groups, 2 * LINE)),
            dma((groups, LINE)),
            dma((groups, LINE)),
            dma((groups, LINE * PLANE)),
            dma((6,)),
            dma((6,)),
            dma((5,)),
        ],
        compiler_params=pltpu.CompilerParams(
            collective_id=0, has_side_effects=True, vmem_limit_bytes=40 * 1024 * 1024
        ),
    )(
        cand_embed[0], hist_keys[0], hist_values[0], in_weight, out_weight,
        norm_gain[None, :], cand_counts, hist_lengths, self_mask[0],
    )
    return out[None]


def on_device(
    cand_embed,
    hist_keys,
    hist_values,
    in_weight,
    out_weight,
    norm_gain,
    cand_counts,
    hist_lengths,
    self_mask,
):
    req_count, cand_count, model_width = cand_embed.shape
    head_dim = model_width // HEADS
    scale_factor = head_dim ** (-0.5)
    flat_rows = cand_embed.reshape(req_count * cand_count, model_width)
    pre_act = jnp.dot(
        flat_rows,
        lax.all_gather(in_weight, "req", axis=0, tiled=True),
        preferred_element_type=jnp.float32,
    )
    projected = (
        jax.nn.silu(pre_act).astype(jnp.bfloat16).reshape(req_count, cand_count, 4 * model_width)
    )
    gate_u = projected[:, :, :model_width]
    self_values = projected[:, :, model_width : 2 * model_width]
    queries = projected[:, :, 2 * model_width : 3 * model_width]
    self_keys = projected[:, :, 3 * model_width :]
    query_heads = queries.reshape(req_count, cand_count, HEADS, head_dim)
    divisor = (hist_lengths + SELF_BLOCK).astype(jnp.float32)
    cand_index = lax.axis_index("hist") * cand_count + jnp.arange(cand_count)
    is_live = cand_index[None, :] < cand_counts[:, None]
    key_part = lax.all_gather(hist_keys, "hist", axis=1, tiled=True)
    value_part = lax.all_gather(hist_values, "hist", axis=1, tiled=True)
    span = key_part.shape[1]
    key_heads = key_part.reshape(req_count, span, HEADS, head_dim)
    value_heads = value_part.reshape(req_count, span, HEADS, head_dim)
    scores = (
        jnp.einsum("rchd,rnhd->rhcn", query_heads, key_heads, preferred_element_type=jnp.float32)
        * scale_factor
    )
    visible = (jnp.arange(span)[None, :] < hist_lengths[:, None]).astype(jnp.float32)
    mixing = (
        jax.nn.silu(scores) * visible[:, None, None, :] / divisor[:, None, None, None]
    ).astype(jnp.bfloat16)
    attended = jnp.einsum(
        "rhcn,rnhd->rchd", mixing, value_heads, preferred_element_type=jnp.float32
    )
    blocks = cand_count // SELF_BLOCK
    query_blocks = queries.reshape(req_count, blocks, SELF_BLOCK, HEADS, head_dim)
    key_blocks = self_keys.reshape(req_count, blocks, SELF_BLOCK, HEADS, head_dim)
    value_blocks = self_values.reshape(req_count, blocks, SELF_BLOCK, HEADS, head_dim)
    self_scores = (
        jnp.einsum(
            "rbphd,rbchd->rbhpc", query_blocks, key_blocks, preferred_element_type=jnp.float32
        )
        * scale_factor
    )
    position = jnp.arange(SELF_BLOCK)
    causal = position[None, :] <= position[:, None]
    diagonal = position[None, :] == position[:, None]
    given = self_mask.reshape(req_count, blocks, SELF_BLOCK, SELF_BLOCK) == 1
    key_live = is_live.reshape(req_count, blocks, 1, SELF_BLOCK)
    allowed = (causal[None, None] & (given | diagonal[None, None]) & key_live).astype(jnp.float32)
    self_mix = (
        jax.nn.silu(self_scores) * allowed[:, :, None, :, :] / divisor[:, None, None, None, None]
    ).astype(jnp.bfloat16)
    self_part = jnp.einsum(
        "rbhpc,rbchd->rbphd", self_mix, value_blocks, preferred_element_type=jnp.float32
    )
    attended = (attended + self_part.reshape(req_count, cand_count, HEADS, head_dim)).reshape(
        req_count, cand_count, model_width
    )
    average = jnp.mean(attended, axis=2, keepdims=True)
    variance = jnp.mean((attended - average) ** 2, axis=2, keepdims=True)
    gated = (
        (attended - average) / jnp.sqrt(variance + 1e-05) * norm_gain * gate_u.astype(jnp.float32)
    ).astype(jnp.bfloat16)
    gated_rows = gated.reshape(req_count * cand_count, model_width)
    branch = jnp.dot(gated_rows, out_weight, preferred_element_type=jnp.float32)
    branch = branch.reshape(req_count, cand_count, model_width)
    result = cand_embed.astype(jnp.float32) + is_live.astype(jnp.float32)[:, :, None] * branch
    return result.astype(jnp.bfloat16)


def solution(mesh):
    in_specs = (
        P("req", "hist", None),
        P("req", "hist", None),
        P("req", "hist", None),
        P("req", None),
        P(),
        P(),
        P("req"),
        P("req"),
        P("req", "hist", None),
    )
    out_specs = P("req", "hist", None)
    paired = mesh.shape["hist"] == 2 and mesh.shape["req"] == LINE * PLANE
    return jax.shard_map(
        on_device_kernel if paired else on_device,
        mesh=mesh, in_specs=in_specs, out_specs=out_specs, check_vma=False,
    )
```

```python
import functools

import jax
import jax.numpy as jnp
from jax import lax
from jax.experimental import pallas as pl
from jax.experimental.pallas import tpu as pltpu
from jax.sharding import PartitionSpec as P

HEADS = 8
SELF_BLOCK = 64
MESH = pl.DeviceIdType.MESH
LINE = 4
PLANE = 4
GROUPS = (2, 3, 1, 0)


def interleave(events, work, start):
    slots = max(len(events) - start, 1)
    done = 0
    for at, event in enumerate(events):
        event()
        if at >= start:
            upto = (at - start + 1) * len(work) // slots
            for job in work[done:upto]:
                job()
            done = max(done, upto)
    for job in work[done:]:
        job()


def silu(x):
    half = x * 0.5
    return half + half * jnp.tanh(half)


def layer_kernel(
    cand_hbm, hk_hbm, hv_hbm, w_ref, wout_hbm, gain_hbm, count_ref, length_ref, mask_ref,
    out_ref,
    gain, cand, hist_k, hist_v, wbuf, wout, mask, amask, q, k, v, att, st_mine, st_other,
    g_mine, g_send, g_recv,
    send_x, send_y, send_up, send_down, recv, sib_send, sib_recv, local_sem,
):
    rows, width = cand_hbm.shape
    all_rows = 2 * rows
    depth = w_ref.shape[0]
    half = width // 2
    hist_rows = hk_hbm.shape[0]
    span = 2 * hist_rows
    heads = HEADS // 2
    head_dim = width // HEADS
    scale = head_dim ** (-0.5)

    me = lax.axis_index("req")
    core = lax.axis_index("hist")
    other = 1 - core
    z = me // PLANE
    plane = me - z * PLANE
    y = plane // 2
    x = plane - 2 * y
    plane_x = 2 * y + (1 - x)
    plane_y = 2 * (1 - y) + x
    plane_d = 2 * (1 - y) + (1 - x)
    to_x = {"req": z * PLANE + plane_x}
    to_y = {"req": z * PLANE + plane_y}
    to_up = {"req": me + PLANE}
    to_down = {"req": me - PLANE}
    sibling = {"hist": other}
    has_up = z < LINE - 1
    has_down = z > 0
    near = z + 1 - 2 * (z // 3)
    far = 3 * (1 - z // 2)
    near_z = (z, near, 6 - z - near - far, far)

    my_cols = pl.ds(pl.multiple_of(core * half, half), half)
    other_cols = pl.ds(pl.multiple_of(other * half, half), half)
    my_rows = pl.ds(pl.multiple_of(core * rows, rows), rows)
    other_rows = pl.ds(pl.multiple_of(other * rows, rows), rows)
    my_hist = pl.ds(pl.multiple_of(core * hist_rows, hist_rows), hist_rows)
    locals_ = [
        pltpu.make_async_copy(cand_hbm, cand.at[my_rows], local_sem.at[0]),
        pltpu.make_async_copy(hk_hbm.at[:, my_cols], hist_k.at[my_hist], local_sem.at[1]),
        pltpu.make_async_copy(hv_hbm.at[:, my_cols], hist_v.at[my_hist], local_sem.at[2]),
        pltpu.make_async_copy(mask_ref, mask.at[core], local_sem.at[3]),
        pltpu.make_async_copy(wout_hbm, wout, local_sem.at[4]),
        pltpu.make_async_copy(gain_hbm, gain, local_sem.at[5]),
    ]
    for g, base in enumerate(GROUPS):
        start = pl.multiple_of(base * width + core * half, half)
        locals_.append(
            pltpu.make_async_copy(
                w_ref.at[:, pl.ds(start, half)],
                wbuf.at[g, pl.ds(pl.multiple_of(me * depth, depth), depth)],
                local_sem.at[6 + g],
            )
        )
    for copy in locals_:
        copy.start()

    barrier = pltpu.get_barrier_semaphore()

    def greet(target):
        pl.semaphore_signal(barrier, inc=1, device_id=target, device_id_type=MESH)

    greet(to_x)
    greet(to_y)
    greet(sibling)
    pl.when(has_up)(lambda: greet(to_up))
    pl.when(has_down)(lambda: greet(to_down))
    pl.semaphore_wait(barrier, 3 + (1 - z // (LINE - 1)) + (z + LINE - 2) // (LINE - 1))

    def slot(g, chip):
        return wbuf.at[g, pl.ds(pl.multiple_of(chip * depth, depth), depth)]

    def remote(src, dst, ssem, rsem, target):
        return pltpu.make_async_remote_copy(
            src_ref=src, dst_ref=dst, send_sem=ssem, recv_sem=rsem,
            device_id=target, device_id_type=MESH,
        )

    def own_piece(g):
        start = pl.multiple_of(GROUPS[g] * width + core * half, half)
        return w_ref.at[:, pl.ds(start, half)]

    def send(g, chip, sem, target, src=None):
        here = slot(g, chip) if src is None else src
        remote(here, slot(g, chip), sem, recv.at[g, chip], target).start()

    def arrived(g, chip):
        remote(slot(g, chip), slot(g, chip), recv.at[g, chip], recv.at[g, chip], to_x).wait_recv()

    def own(g):
        src = own_piece(g)
        send(g, me, send_x.at[g, z], to_x, src)
        send(g, me, send_y.at[g, z], to_y, src)
        pl.when(has_up)(lambda: send(g, me, send_up.at[g, z], to_up, src))
        pl.when(has_down)(lambda: send(g, me, send_down.at[g, z], to_down, src))

    def from_line(g, offset):
        at = z + offset
        chip = me + offset * PLANE

        def body():
            arrived(g, chip)
            if offset < 0:
                pl.when(has_up)(lambda: send(g, chip, send_up.at[g, at], to_up))
            else:
                pl.when(has_down)(lambda: send(g, chip, send_down.at[g, at], to_down))
            send(g, chip, send_x.at[g, at], to_x)
            send(g, chip, send_y.at[g, at], to_y)

        pl.when((at >= 0) if offset < 0 else (at < LINE))(body)

    def from_sides(g, step):
        at = near_z[step]
        even = at % 2 == 0
        chip_x = at * PLANE + plane_x
        chip_y = at * PLANE + plane_y
        arrived(g, chip_x)
        pl.when(even)(lambda: send(g, chip_x, send_y.at[g, LINE + at], to_y))
        arrived(g, chip_y)
        pl.when(jnp.logical_not(even))(
            lambda: send(g, chip_y, send_x.at[g, LINE + at], to_x)
        )

    def from_diagonal(g):
        for at in near_z:
            arrived(g, at * PLANE + plane_d)

    def forwards(g):
        part = functools.partial
        events = [part(from_line, g, -1), part(from_line, g, 1), part(from_sides, g, 0)]
        events += [part(from_line, g, -2), part(from_line, g, 2)]
        events += [part(from_sides, g, 1), part(from_sides, g, 2)]
        events += [part(from_line, g, -3), part(from_line, g, 3)]
        if g + 1 < len(GROUPS):
            events += [part(own, g + 1)]
        events += [part(from_sides, g, 3)]
        return events

    own(0)

    sib = [
        remote(cand_hbm, cand.at[my_rows], sib_send.at[0], sib_recv.at[0], sibling),
        remote(hk_hbm.at[:, other_cols], hist_k.at[my_hist], sib_send.at[1], sib_recv.at[1], sibling),
        remote(hv_hbm.at[:, other_cols], hist_v.at[my_hist], sib_send.at[2], sib_recv.at[2], sibling),
        remote(mask_ref, mask.at[core], sib_send.at[3], sib_recv.at[3], sibling),
    ]
    for copy in sib:
        copy.start()

    count = count_ref[0]
    length = length_ref[0]
    divisor = (length + SELF_BLOCK).astype(jnp.float32)

    def inputs_here():
        for copy in locals_:
            copy.wait()
        for copy in sib:
            copy.wait_recv()

    tile = 2 * SELF_BLOCK
    tiles = all_rows // tile

    def make_mask(t):
        r0 = t * tile
        row = lax.broadcasted_iota(jnp.int32, (tile, tile), 0)
        col = lax.broadcasted_iota(jnp.int32, (tile, tile), 1)
        given = mask[r0 // rows, :, pl.ds(r0 % rows, tile)]
        given = jnp.concatenate([given, given], axis=0).T
        keep = (
            (row // SELF_BLOCK == col // SELF_BLOCK)
            & (col <= row)
            & ((given == 1) | (row == col))
            & (r0 + col < count)
        )
        amask[pl.ds(r0, tile), :] = jnp.where(keep, 1.0 / divisor, 0.0)

    def masks():
        for t in range(tiles):
            make_mask(t)

    cols = half // 2

    def project(g, dst, r, n):
        acc = jnp.dot(
            cand[pl.ds(r * rows, rows), :],
            wbuf[g, :, pl.ds(n * cols, cols)],
            preferred_element_type=jnp.float32,
        )
        dst[pl.ds(r * rows, rows), pl.ds(n * cols, cols)] = silu(acc).astype(jnp.bfloat16)

    def projections(g, dst):
        return [functools.partial(project, g, dst, r, n) for n in range(2) for r in range(2)]

    nt = (((1,), (1,)), ((), ()))

    def hist_part(t):
        r0 = t * tile
        col = lax.broadcasted_iota(jnp.int32, (1, span), 1)
        weight = jnp.where(col < length, 1.0 / divisor, 0.0)
        for h in range(heads):
            hc = slice(h * head_dim, (h + 1) * head_dim)
            s = lax.dot_general(
                q[pl.ds(r0, tile), hc], hist_k[:, hc], nt, preferred_element_type=jnp.float32
            )
            mix = (silu(s * scale) * weight).astype(jnp.bfloat16)
            att[pl.ds(r0, tile), hc] = jnp.dot(
                mix, hist_v[:, hc], preferred_element_type=jnp.float32
            )

    def self_part(t):
        r0 = t * tile
        for h in range(heads):
            hc = slice(h * head_dim, (h + 1) * head_dim)
            s = lax.dot_general(
                q[pl.ds(r0, tile), hc], k[pl.ds(r0, tile), hc], nt,
                preferred_element_type=jnp.float32,
            )
            mix = (silu(s * scale) * amask[pl.ds(r0, tile), :]).astype(jnp.bfloat16)
            att[pl.ds(r0, tile), hc] += jnp.dot(
                mix, v[pl.ds(r0, tile), hc], preferred_element_type=jnp.float32
            )
        here = att[pl.ds(r0, tile), :]
        mean = jnp.mean(here, axis=1, keepdims=True)
        spread = jnp.sum((here - mean) ** 2, axis=1, keepdims=True)
        lane = lax.broadcasted_iota(jnp.int32, (tile, 128), 1)
        st_mine[pl.ds(r0, tile), :] = jnp.where(lane < 64, mean, spread)

    stats = remote(st_mine, st_other, sib_send.at[4], sib_recv.at[4], sibling)

    def normalise(t):
        r0 = t * tile
        mine, theirs = st_mine[pl.ds(r0, tile), :], st_other[pl.ds(r0, tile), :]
        mean_a, mean_b = mine[:, 0:1], theirs[:, 0:1]
        gap = mean_a - mean_b
        mean = 0.5 * (mean_a + mean_b)
        variance = (mine[:, 64:65] + theirs[:, 64:65] + gap * gap * (half / 2)) / width
        factor = lax.rsqrt(variance + 1e-05)
        att[pl.ds(r0, tile), :] = (
            (att[pl.ds(r0, tile), :] - mean) * factor * gain[:, my_cols]
        )

    part = functools.partial
    interleave(forwards(0), [], 0)
    inputs_here()
    masks()
    interleave(
        forwards(1)[:4] + [part(from_diagonal, 0)] + forwards(1)[4:], projections(0, q), 4
    )
    work = projections(1, k) + [part(hist_part, t) for t in range(tiles)]
    interleave(forwards(2)[:4] + [part(from_diagonal, 1)] + forwards(2)[4:], work, 4)
    work = projections(2, v) + [part(self_part, t) for t in range(tiles)]
    work += [stats.start]
    interleave(forwards(3)[:4] + [part(from_diagonal, 2)] + forwards(3)[4:], work, 4)
    stats.wait_recv()
    for t in range(tiles):
        normalise(t)

    def gate(dst, at):
        for n in range(2):
            nc = pl.ds(n * cols, cols)
            acc = jnp.dot(
                cand[at, :], wbuf[3, :, nc], preferred_element_type=jnp.float32
            )
            u = silu(acc).astype(jnp.bfloat16).astype(jnp.float32)
            dst[:, nc] = (att[at, nc] * u).astype(jnp.bfloat16)

    from_diagonal(3)
    gate(g_send, other_rows)
    gated = remote(g_send, g_recv, sib_send.at[5], sib_recv.at[5], sibling)
    gated.start()
    gate(g_mine, my_rows)
    live_row = core * rows + lax.broadcasted_iota(jnp.int32, (rows, 1), 0)
    live = jnp.where(live_row < count, 1.0, 0.0)
    for n in range(4):
        nc = slice(n * 256, (n + 1) * 256)
        att_cols = pl.ds((n % 2) * 256, 256)
        att[pl.ds((n // 2) * rows, rows), att_cols] = jnp.dot(
            g_mine[...], wout[my_cols, nc], preferred_element_type=jnp.float32
        )
    gated.wait_recv()
    for n in range(4):
        nc = slice(n * 256, (n + 1) * 256)
        att_cols = pl.ds((n % 2) * 256, 256)
        branch = att[pl.ds((n // 2) * rows, rows), att_cols] + jnp.dot(
            g_recv[...], wout[other_cols, nc], preferred_element_type=jnp.float32
        )
        res = cand[my_rows, nc].astype(jnp.float32) + live * branch
        out_ref[:, nc] = res.astype(jnp.bfloat16)

    for copy in sib:
        copy.wait_send()
    stats.wait_send()
    gated.wait_send()

    def left(sem):
        piece = slot(0, 0)
        remote(piece, piece, sem, sem, to_x).wait_send()

    for g in range(len(GROUPS)):
        for at in range(LINE):
            left(send_x.at[g, at])
            left(send_y.at[g, at])
            if at % 2 == 0:
                left(send_y.at[g, LINE + at])
            else:
                left(send_x.at[g, LINE + at])
            pl.when(has_up & (at <= z))(lambda: left(send_up.at[g, at]))
            pl.when(has_down & (at >= z))(lambda: left(send_down.at[g, at]))


def on_device_kernel(
    cand_embed, hist_keys, hist_values, in_weight, out_weight, norm_gain,
    cand_counts, hist_lengths, self_mask,
):
    _, rows, width = cand_embed.shape
    hist_rows = hist_keys.shape[1]
    half = width // 2
    depth = in_weight.shape[0]
    bf16, f32 = jnp.bfloat16, jnp.float32
    groups = len(GROUPS)
    vmem = pl.BlockSpec(memory_space=pltpu.VMEM)
    smem = pl.BlockSpec(memory_space=pltpu.SMEM)
    hbm = pl.BlockSpec(memory_space=pl.ANY)
    dma = pltpu.SemaphoreType.DMA
    out = pl.pallas_call(
        layer_kernel,
        out_shape=jax.ShapeDtypeStruct((rows, width), bf16),
        in_specs=[hbm, hbm, hbm, hbm, hbm, hbm, smem, smem, hbm],
        out_specs=vmem,
        scratch_shapes=[
            pltpu.VMEM((1, width), f32),
            pltpu.VMEM((2 * rows, width), bf16),
            pltpu.VMEM((2 * hist_rows, half), bf16),
            pltpu.VMEM((2 * hist_rows, half), bf16),
            pltpu.VMEM((groups, width, half), bf16),
            pltpu.VMEM((width, width), bf16),
            pltpu.VMEM((2, SELF_BLOCK, rows), jnp.int32),
            pltpu.VMEM((2 * rows, 2 * SELF_BLOCK), f32),
            pltpu.VMEM((2 * rows, half), bf16),
            pltpu.VMEM((2 * rows, half), bf16),
            pltpu.VMEM((2 * rows, half), bf16),
            pltpu.VMEM((2 * rows, half), f32),
            pltpu.VMEM((2 * rows, 128), f32),
            pltpu.VMEM((2 * rows, 128), f32),
            pltpu.VMEM((rows, half), bf16),
            pltpu.VMEM((rows, half), bf16),
            pltpu.VMEM((rows, half), bf16),
            dma((groups, 2 * LINE)),
            dma((groups, 2 * LINE)),
            dma((groups, LINE)),
            dma((groups, LINE)),
            dma((groups, LINE * PLANE)),
            dma((6,)),
            dma((6,)),
            dma((6 + groups,)),
        ],
        compiler_params=pltpu.CompilerParams(
            collective_id=0, has_side_effects=True, vmem_limit_bytes=60 * 1024 * 1024
        ),
    )(
        cand_embed[0], hist_keys[0], hist_values[0], in_weight, out_weight,
        norm_gain[None, :], cand_counts, hist_lengths, self_mask[0].T,
    )
    return out[None]


def on_device(
    cand_embed,
    hist_keys,
    hist_values,
    in_weight,
    out_weight,
    norm_gain,
    cand_counts,
    hist_lengths,
    self_mask,
):
    req_count, cand_count, model_width = cand_embed.shape
    head_dim = model_width // HEADS
    scale_factor = head_dim ** (-0.5)
    flat_rows = cand_embed.reshape(req_count * cand_count, model_width)
    pre_act = jnp.dot(
        flat_rows,
        lax.all_gather(in_weight, "req", axis=0, tiled=True),
        preferred_element_type=jnp.float32,
    )
    projected = (
        jax.nn.silu(pre_act).astype(jnp.bfloat16).reshape(req_count, cand_count, 4 * model_width)
    )
    gate_u = projected[:, :, :model_width]
    self_values = projected[:, :, model_width : 2 * model_width]
    queries = projected[:, :, 2 * model_width : 3 * model_width]
    self_keys = projected[:, :, 3 * model_width :]
    query_heads = queries.reshape(req_count, cand_count, HEADS, head_dim)
    divisor = (hist_lengths + SELF_BLOCK).astype(jnp.float32)
    cand_index = lax.axis_index("hist") * cand_count + jnp.arange(cand_count)
    is_live = cand_index[None, :] < cand_counts[:, None]
    key_part = lax.all_gather(hist_keys, "hist", axis=1, tiled=True)
    value_part = lax.all_gather(hist_values, "hist", axis=1, tiled=True)
    span = key_part.shape[1]
    key_heads = key_part.reshape(req_count, span, HEADS, head_dim)
    value_heads = value_part.reshape(req_count, span, HEADS, head_dim)
    scores = (
        jnp.einsum("rchd,rnhd->rhcn", query_heads, key_heads, preferred_element_type=jnp.float32)
        * scale_factor
    )
    visible = (jnp.arange(span)[None, :] < hist_lengths[:, None]).astype(jnp.float32)
    mixing = (
        jax.nn.silu(scores) * visible[:, None, None, :] / divisor[:, None, None, None]
    ).astype(jnp.bfloat16)
    attended = jnp.einsum(
        "rhcn,rnhd->rchd", mixing, value_heads, preferred_element_type=jnp.float32
    )
    blocks = cand_count // SELF_BLOCK
    query_blocks = queries.reshape(req_count, blocks, SELF_BLOCK, HEADS, head_dim)
    key_blocks = self_keys.reshape(req_count, blocks, SELF_BLOCK, HEADS, head_dim)
    value_blocks = self_values.reshape(req_count, blocks, SELF_BLOCK, HEADS, head_dim)
    self_scores = (
        jnp.einsum(
            "rbphd,rbchd->rbhpc", query_blocks, key_blocks, preferred_element_type=jnp.float32
        )
        * scale_factor
    )
    position = jnp.arange(SELF_BLOCK)
    causal = position[None, :] <= position[:, None]
    diagonal = position[None, :] == position[:, None]
    given = self_mask.reshape(req_count, blocks, SELF_BLOCK, SELF_BLOCK) == 1
    key_live = is_live.reshape(req_count, blocks, 1, SELF_BLOCK)
    allowed = (causal[None, None] & (given | diagonal[None, None]) & key_live).astype(jnp.float32)
    self_mix = (
        jax.nn.silu(self_scores) * allowed[:, :, None, :, :] / divisor[:, None, None, None, None]
    ).astype(jnp.bfloat16)
    self_part = jnp.einsum(
        "rbhpc,rbchd->rbphd", self_mix, value_blocks, preferred_element_type=jnp.float32
    )
    attended = (attended + self_part.reshape(req_count, cand_count, HEADS, head_dim)).reshape(
        req_count, cand_count, model_width
    )
    average = jnp.mean(attended, axis=2, keepdims=True)
    variance = jnp.mean((attended - average) ** 2, axis=2, keepdims=True)
    gated = (
        (attended - average) / jnp.sqrt(variance + 1e-05) * norm_gain * gate_u.astype(jnp.float32)
    ).astype(jnp.bfloat16)
    gated_rows = gated.reshape(req_count * cand_count, model_width)
    branch = jnp.dot(gated_rows, out_weight, preferred_element_type=jnp.float32)
    branch = branch.reshape(req_count, cand_count, model_width)
    result = cand_embed.astype(jnp.float32) + is_live.astype(jnp.float32)[:, :, None] * branch
    return result.astype(jnp.bfloat16)


def solution(mesh):
    in_specs = (
        P("req", "hist", None),
        P("req", "hist", None),
        P("req", "hist", None),
        P("req", None),
        P(),
        P(),
        P("req"),
        P("req"),
        P("req", "hist", None),
    )
    out_specs = P("req", "hist", None)
    paired = mesh.shape["hist"] == 2 and mesh.shape["req"] == LINE * PLANE
    return jax.shard_map(
        on_device_kernel if paired else on_device,
        mesh=mesh, in_specs=in_specs, out_specs=out_specs, check_vma=False,
    )
```

```python
import functools

import jax
import jax.numpy as jnp
from jax import lax
from jax.experimental import pallas as pl
from jax.experimental.pallas import tpu as pltpu
from jax.sharding import PartitionSpec as P

HEADS = 8
SELF_BLOCK = 64
MESH = pl.DeviceIdType.MESH
LINE = 4
PLANE = 4
GROUPS = (2, 3, 1, 0)


def interleave(events, work, start):
    slots = max(len(events) - start, 1)
    done = 0
    for at, event in enumerate(events):
        event()
        if at >= start:
            upto = (at - start + 1) * len(work) // slots
            for job in work[done:upto]:
                job()
            done = max(done, upto)
    for job in work[done:]:
        job()


def silu(x):
    half = x * 0.5
    return half + half * jnp.tanh(half)


def layer_kernel(
    cand_hbm, hk_hbm, hv_hbm, w_ref, wout_hbm, gain_hbm, count_ref, length_ref, mask_ref,
    out_ref,
    gain, cand, hist_k, hist_v, wbuf, wout, mask, amask, q, k, v, att, st_mine, st_other,
    g_mine, g_send, g_recv,
    send_x, send_y, send_up, send_down, recv, sib_send, sib_recv, local_sem,
):
    rows, width = cand_hbm.shape
    all_rows = 2 * rows
    depth = w_ref.shape[0]
    half = width // 2
    hist_rows = hk_hbm.shape[0]
    span = 2 * hist_rows
    heads = HEADS // 2
    head_dim = width // HEADS
    scale = head_dim ** (-0.5)

    me = lax.axis_index("req")
    core = lax.axis_index("hist")
    other = 1 - core
    z = me // PLANE
    plane = me - z * PLANE
    y = plane // 2
    x = plane - 2 * y
    plane_x = 2 * y + (1 - x)
    plane_y = 2 * (1 - y) + x
    plane_d = 2 * (1 - y) + (1 - x)
    to_x = {"req": z * PLANE + plane_x}
    to_y = {"req": z * PLANE + plane_y}
    to_up = {"req": me + PLANE}
    to_down = {"req": me - PLANE}
    sibling = {"hist": other}
    has_up = z < LINE - 1
    has_down = z > 0
    near = z + 1 - 2 * (z // 3)
    far = 3 * (1 - z // 2)
    near_z = (z, near, 6 - z - near - far, far)

    my_cols = pl.ds(pl.multiple_of(core * half, half), half)
    other_cols = pl.ds(pl.multiple_of(other * half, half), half)
    my_rows = pl.ds(pl.multiple_of(core * rows, rows), rows)
    other_rows = pl.ds(pl.multiple_of(other * rows, rows), rows)
    my_hist = pl.ds(pl.multiple_of(core * hist_rows, hist_rows), hist_rows)
    locals_ = [
        pltpu.make_async_copy(cand_hbm, cand.at[my_rows], local_sem.at[0]),
        pltpu.make_async_copy(hk_hbm.at[:, my_cols], hist_k.at[my_hist], local_sem.at[1]),
        pltpu.make_async_copy(hv_hbm.at[:, my_cols], hist_v.at[my_hist], local_sem.at[2]),
        pltpu.make_async_copy(mask_ref, mask.at[core], local_sem.at[3]),
        pltpu.make_async_copy(wout_hbm, wout, local_sem.at[4]),
        pltpu.make_async_copy(gain_hbm, gain, local_sem.at[5]),
    ]
    for g, base in enumerate(GROUPS):
        start = pl.multiple_of(base * width + core * half, half)
        locals_.append(
            pltpu.make_async_copy(
                w_ref.at[:, pl.ds(start, half)],
                wbuf.at[g, pl.ds(pl.multiple_of(me * depth, depth), depth)],
                local_sem.at[6 + g],
            )
        )
    for copy in locals_:
        copy.start()

    barrier = pltpu.get_barrier_semaphore()

    def greet(target):
        pl.semaphore_signal(barrier, inc=1, device_id=target, device_id_type=MESH)

    greet(to_x)
    greet(to_y)
    greet(sibling)
    pl.when(has_up)(lambda: greet(to_up))
    pl.when(has_down)(lambda: greet(to_down))
    pl.semaphore_wait(barrier, 3 + (1 - z // (LINE - 1)) + (z + LINE - 2) // (LINE - 1))

    def slot(g, chip):
        return wbuf.at[g, pl.ds(pl.multiple_of(chip * depth, depth), depth)]

    def remote(src, dst, ssem, rsem, target):
        return pltpu.make_async_remote_copy(
            src_ref=src, dst_ref=dst, send_sem=ssem, recv_sem=rsem,
            device_id=target, device_id_type=MESH,
        )

    def own_piece(g):
        start = pl.multiple_of(GROUPS[g] * width + core * half, half)
        return w_ref.at[:, pl.ds(start, half)]

    def send(g, chip, sem, target, src=None):
        here = slot(g, chip) if src is None else src
        remote(here, slot(g, chip), sem, recv.at[g, chip], target).start()

    def arrived(g, chip):
        remote(slot(g, chip), slot(g, chip), recv.at[g, chip], recv.at[g, chip], to_x).wait_recv()

    def own(g):
        src = own_piece(g)
        send(g, me, send_x.at[g, z], to_x, src)
        send(g, me, send_y.at[g, z], to_y, src)
        pl.when(has_up)(lambda: send(g, me, send_up.at[g, z], to_up, src))
        pl.when(has_down)(lambda: send(g, me, send_down.at[g, z], to_down, src))

    def from_line(g, offset):
        at = z + offset
        chip = me + offset * PLANE

        def body():
            arrived(g, chip)
            if offset < 0:
                pl.when(has_up)(lambda: send(g, chip, send_up.at[g, at], to_up))
            else:
                pl.when(has_down)(lambda: send(g, chip, send_down.at[g, at], to_down))
            send(g, chip, send_x.at[g, at], to_x)
            send(g, chip, send_y.at[g, at], to_y)

        pl.when((at >= 0) if offset < 0 else (at < LINE))(body)

    def from_sides(g, step):
        at = near_z[step]
        passed_on = (at % (LINE - 1) == 0) | (at == z)
        even = (at + g) % 2 == 0
        chip_x = at * PLANE + plane_x
        chip_y = at * PLANE + plane_y
        arrived(g, chip_x)
        pl.when(passed_on & even)(lambda: send(g, chip_x, send_y.at[g, LINE + at], to_y))
        arrived(g, chip_y)
        pl.when(passed_on & jnp.logical_not(even))(
            lambda: send(g, chip_y, send_x.at[g, LINE + at], to_x)
        )

    def from_corner(g, step):
        at = near_z[step]
        chip = at * PLANE + plane_d
        inner = at % (LINE - 1) != 0
        arrived(g, chip)
        pl.when(inner & has_up & (z >= at))(
            lambda: send(g, chip, send_up.at[g, LINE + at], to_up)
        )
        pl.when(inner & has_down & (z <= at))(
            lambda: send(g, chip, send_down.at[g, LINE + at], to_down)
        )

    def from_diagonal(g):
        from_corner(g, 2)
        from_corner(g, 3)

    def forwards(g):
        part = functools.partial
        events = [part(from_line, g, -1), part(from_line, g, 1), part(from_sides, g, 0)]
        events += [part(from_line, g, -2), part(from_line, g, 2)]
        events += [part(from_sides, g, 1), part(from_sides, g, 2)]
        events += [part(from_corner, g, 0)]
        events += [part(from_line, g, -3), part(from_line, g, 3)]
        if g + 1 < len(GROUPS):
            events += [part(own, g + 1)]
        events += [part(from_sides, g, 3), part(from_corner, g, 1)]
        return events

    own(0)

    sib = [
        remote(cand_hbm, cand.at[my_rows], sib_send.at[0], sib_recv.at[0], sibling),
        remote(hk_hbm.at[:, other_cols], hist_k.at[my_hist], sib_send.at[1], sib_recv.at[1], sibling),
        remote(hv_hbm.at[:, other_cols], hist_v.at[my_hist], sib_send.at[2], sib_recv.at[2], sibling),
        remote(mask_ref, mask.at[core], sib_send.at[3], sib_recv.at[3], sibling),
    ]
    for copy in sib:
        copy.start()

    count = count_ref[0]
    length = length_ref[0]
    divisor = (length + SELF_BLOCK).astype(jnp.float32)

    def inputs_here():
        for copy in locals_:
            copy.wait()
        for copy in sib:
            copy.wait_recv()

    tile = 2 * SELF_BLOCK
    tiles = all_rows // tile

    def make_mask(t):
        r0 = t * tile
        row = lax.broadcasted_iota(jnp.int32, (tile, tile), 0)
        col = lax.broadcasted_iota(jnp.int32, (tile, tile), 1)
        given = mask[r0 // rows, :, pl.ds(r0 % rows, tile)]
        given = jnp.concatenate([given, given], axis=0).T
        keep = (
            (row // SELF_BLOCK == col // SELF_BLOCK)
            & (col <= row)
            & ((given == 1) | (row == col))
            & (r0 + col < count)
        )
        amask[pl.ds(r0, tile), :] = jnp.where(keep, 1.0 / divisor, 0.0)

    def masks():
        for t in range(tiles):
            make_mask(t)

    cols = half // 2

    def project(g, dst, r, n):
        acc = jnp.dot(
            cand[pl.ds(r * rows, rows), :],
            wbuf[g, :, pl.ds(n * cols, cols)],
            preferred_element_type=jnp.float32,
        )
        dst[pl.ds(r * rows, rows), pl.ds(n * cols, cols)] = silu(acc).astype(jnp.bfloat16)

    def projections(g, dst):
        return [functools.partial(project, g, dst, r, n) for n in range(2) for r in range(2)]

    nt = (((1,), (1,)), ((), ()))

    def hist_part(t):
        r0 = t * tile
        col = lax.broadcasted_iota(jnp.int32, (1, span), 1)
        weight = jnp.where(col < length, 1.0 / divisor, 0.0)
        for h in range(heads):
            hc = slice(h * head_dim, (h + 1) * head_dim)
            s = lax.dot_general(
                q[pl.ds(r0, tile), hc], hist_k[:, hc], nt, preferred_element_type=jnp.float32
            )
            mix = (silu(s * scale) * weight).astype(jnp.bfloat16)
            att[pl.ds(r0, tile), hc] = jnp.dot(
                mix, hist_v[:, hc], preferred_element_type=jnp.float32
            )

    def self_part(t):
        r0 = t * tile
        for h in range(heads):
            hc = slice(h * head_dim, (h + 1) * head_dim)
            s = lax.dot_general(
                q[pl.ds(r0, tile), hc], k[pl.ds(r0, tile), hc], nt,
                preferred_element_type=jnp.float32,
            )
            mix = (silu(s * scale) * amask[pl.ds(r0, tile), :]).astype(jnp.bfloat16)
            att[pl.ds(r0, tile), hc] += jnp.dot(
                mix, v[pl.ds(r0, tile), hc], preferred_element_type=jnp.float32
            )
        here = att[pl.ds(r0, tile), :]
        mean = jnp.mean(here, axis=1, keepdims=True)
        spread = jnp.sum((here - mean) ** 2, axis=1, keepdims=True)
        lane = lax.broadcasted_iota(jnp.int32, (tile, 128), 1)
        st_mine[pl.ds(r0, tile), :] = jnp.where(lane < 64, mean, spread)

    stats = remote(st_mine, st_other, sib_send.at[4], sib_recv.at[4], sibling)

    def normalise(t):
        r0 = t * tile
        mine, theirs = st_mine[pl.ds(r0, tile), :], st_other[pl.ds(r0, tile), :]
        mean_a, mean_b = mine[:, 0:1], theirs[:, 0:1]
        gap = mean_a - mean_b
        mean = 0.5 * (mean_a + mean_b)
        variance = (mine[:, 64:65] + theirs[:, 64:65] + gap * gap * (half / 2)) / width
        factor = lax.rsqrt(variance + 1e-05)
        att[pl.ds(r0, tile), :] = (
            (att[pl.ds(r0, tile), :] - mean) * factor * gain[:, my_cols]
        )

    part = functools.partial
    interleave(forwards(0), [], 0)
    inputs_here()
    masks()
    interleave(
        forwards(1)[:4] + [part(from_diagonal, 0)] + forwards(1)[4:], projections(0, q), 4
    )
    work = projections(1, k) + [part(hist_part, t) for t in range(tiles)]
    interleave(forwards(2)[:4] + [part(from_diagonal, 1)] + forwards(2)[4:], work, 4)
    work = projections(2, v) + [part(self_part, t) for t in range(tiles)]
    work += [stats.start]
    interleave(forwards(3)[:4] + [part(from_diagonal, 2)] + forwards(3)[4:], work, 4)
    stats.wait_recv()
    for t in range(tiles):
        normalise(t)

    def gate(dst, at):
        for n in range(2):
            nc = pl.ds(n * cols, cols)
            acc = jnp.dot(
                cand[at, :], wbuf[3, :, nc], preferred_element_type=jnp.float32
            )
            u = silu(acc).astype(jnp.bfloat16).astype(jnp.float32)
            dst[:, nc] = (att[at, nc] * u).astype(jnp.bfloat16)

    from_diagonal(3)
    gate(g_send, other_rows)
    gated = remote(g_send, g_recv, sib_send.at[5], sib_recv.at[5], sibling)
    gated.start()
    gate(g_mine, my_rows)
    live_row = core * rows + lax.broadcasted_iota(jnp.int32, (rows, 1), 0)
    live = jnp.where(live_row < count, 1.0, 0.0)
    for n in range(4):
        nc = slice(n * 256, (n + 1) * 256)
        att_cols = pl.ds((n % 2) * 256, 256)
        att[pl.ds((n // 2) * rows, rows), att_cols] = jnp.dot(
            g_mine[...], wout[my_cols, nc], preferred_element_type=jnp.float32
        )
    gated.wait_recv()
    for n in range(4):
        nc = slice(n * 256, (n + 1) * 256)
        att_cols = pl.ds((n % 2) * 256, 256)
        branch = att[pl.ds((n // 2) * rows, rows), att_cols] + jnp.dot(
            g_recv[...], wout[other_cols, nc], preferred_element_type=jnp.float32
        )
        res = cand[my_rows, nc].astype(jnp.float32) + live * branch
        out_ref[:, nc] = res.astype(jnp.bfloat16)

    for copy in sib:
        copy.wait_send()
    stats.wait_send()
    gated.wait_send()

    def left(sem):
        piece = slot(0, 0)
        remote(piece, piece, sem, sem, to_x).wait_send()

    for g in range(len(GROUPS)):
        for at in range(LINE):
            left(send_x.at[g, at])
            left(send_y.at[g, at])
            passed_on = at % (LINE - 1) == 0
            side = send_y if (at + g) % 2 == 0 else send_x
            if passed_on:
                left(side.at[g, LINE + at])
            else:
                pl.when(z == at)(lambda: left(side.at[g, LINE + at]))
                pl.when(has_up & (z >= at))(lambda: left(send_up.at[g, LINE + at]))
                pl.when(has_down & (z <= at))(lambda: left(send_down.at[g, LINE + at]))
            pl.when(has_up & (at <= z))(lambda: left(send_up.at[g, at]))
            pl.when(has_down & (at >= z))(lambda: left(send_down.at[g, at]))


def on_device_kernel(
    cand_embed, hist_keys, hist_values, in_weight, out_weight, norm_gain,
    cand_counts, hist_lengths, self_mask,
):
    _, rows, width = cand_embed.shape
    hist_rows = hist_keys.shape[1]
    half = width // 2
    depth = in_weight.shape[0]
    bf16, f32 = jnp.bfloat16, jnp.float32
    groups = len(GROUPS)
    vmem = pl.BlockSpec(memory_space=pltpu.VMEM)
    smem = pl.BlockSpec(memory_space=pltpu.SMEM)
    hbm = pl.BlockSpec(memory_space=pl.ANY)
    dma = pltpu.SemaphoreType.DMA
    out = pl.pallas_call(
        layer_kernel,
        out_shape=jax.ShapeDtypeStruct((rows, width), bf16),
        in_specs=[hbm, hbm, hbm, hbm, hbm, hbm, smem, smem, hbm],
        out_specs=vmem,
        scratch_shapes=[
            pltpu.VMEM((1, width), f32),
            pltpu.VMEM((2 * rows, width), bf16),
            pltpu.VMEM((2 * hist_rows, half), bf16),
            pltpu.VMEM((2 * hist_rows, half), bf16),
            pltpu.VMEM((groups, width, half), bf16),
            pltpu.VMEM((width, width), bf16),
            pltpu.VMEM((2, SELF_BLOCK, rows), jnp.int32),
            pltpu.VMEM((2 * rows, 2 * SELF_BLOCK), f32),
            pltpu.VMEM((2 * rows, half), bf16),
            pltpu.VMEM((2 * rows, half), bf16),
            pltpu.VMEM((2 * rows, half), bf16),
            pltpu.VMEM((2 * rows, half), f32),
            pltpu.VMEM((2 * rows, 128), f32),
            pltpu.VMEM((2 * rows, 128), f32),
            pltpu.VMEM((rows, half), bf16),
            pltpu.VMEM((rows, half), bf16),
            pltpu.VMEM((rows, half), bf16),
            dma((groups, 2 * LINE)),
            dma((groups, 2 * LINE)),
            dma((groups, 2 * LINE)),
            dma((groups, 2 * LINE)),
            dma((groups, LINE * PLANE)),
            dma((6,)),
            dma((6,)),
            dma((6 + groups,)),
        ],
        compiler_params=pltpu.CompilerParams(
            collective_id=0, has_side_effects=True, vmem_limit_bytes=60 * 1024 * 1024
        ),
    )(
        cand_embed[0], hist_keys[0], hist_values[0], in_weight, out_weight,
        norm_gain[None, :], cand_counts, hist_lengths, self_mask[0].T,
    )
    return out[None]


def on_device(
    cand_embed,
    hist_keys,
    hist_values,
    in_weight,
    out_weight,
    norm_gain,
    cand_counts,
    hist_lengths,
    self_mask,
):
    req_count, cand_count, model_width = cand_embed.shape
    head_dim = model_width // HEADS
    scale_factor = head_dim ** (-0.5)
    flat_rows = cand_embed.reshape(req_count * cand_count, model_width)
    pre_act = jnp.dot(
        flat_rows,
        lax.all_gather(in_weight, "req", axis=0, tiled=True),
        preferred_element_type=jnp.float32,
    )
    projected = (
        jax.nn.silu(pre_act).astype(jnp.bfloat16).reshape(req_count, cand_count, 4 * model_width)
    )
    gate_u = projected[:, :, :model_width]
    self_values = projected[:, :, model_width : 2 * model_width]
    queries = projected[:, :, 2 * model_width : 3 * model_width]
    self_keys = projected[:, :, 3 * model_width :]
    query_heads = queries.reshape(req_count, cand_count, HEADS, head_dim)
    divisor = (hist_lengths + SELF_BLOCK).astype(jnp.float32)
    cand_index = lax.axis_index("hist") * cand_count + jnp.arange(cand_count)
    is_live = cand_index[None, :] < cand_counts[:, None]
    key_part = lax.all_gather(hist_keys, "hist", axis=1, tiled=True)
    value_part = lax.all_gather(hist_values, "hist", axis=1, tiled=True)
    span = key_part.shape[1]
    key_heads = key_part.reshape(req_count, span, HEADS, head_dim)
    value_heads = value_part.reshape(req_count, span, HEADS, head_dim)
    scores = (
        jnp.einsum("rchd,rnhd->rhcn", query_heads, key_heads, preferred_element_type=jnp.float32)
        * scale_factor
    )
    visible = (jnp.arange(span)[None, :] < hist_lengths[:, None]).astype(jnp.float32)
    mixing = (
        jax.nn.silu(scores) * visible[:, None, None, :] / divisor[:, None, None, None]
    ).astype(jnp.bfloat16)
    attended = jnp.einsum(
        "rhcn,rnhd->rchd", mixing, value_heads, preferred_element_type=jnp.float32
    )
    blocks = cand_count // SELF_BLOCK
    query_blocks = queries.reshape(req_count, blocks, SELF_BLOCK, HEADS, head_dim)
    key_blocks = self_keys.reshape(req_count, blocks, SELF_BLOCK, HEADS, head_dim)
    value_blocks = self_values.reshape(req_count, blocks, SELF_BLOCK, HEADS, head_dim)
    self_scores = (
        jnp.einsum(
            "rbphd,rbchd->rbhpc", query_blocks, key_blocks, preferred_element_type=jnp.float32
        )
        * scale_factor
    )
    position = jnp.arange(SELF_BLOCK)
    causal = position[None, :] <= position[:, None]
    diagonal = position[None, :] == position[:, None]
    given = self_mask.reshape(req_count, blocks, SELF_BLOCK, SELF_BLOCK) == 1
    key_live = is_live.reshape(req_count, blocks, 1, SELF_BLOCK)
    allowed = (causal[None, None] & (given | diagonal[None, None]) & key_live).astype(jnp.float32)
    self_mix = (
        jax.nn.silu(self_scores) * allowed[:, :, None, :, :] / divisor[:, None, None, None, None]
    ).astype(jnp.bfloat16)
    self_part = jnp.einsum(
        "rbhpc,rbchd->rbphd", self_mix, value_blocks, preferred_element_type=jnp.float32
    )
    attended = (attended + self_part.reshape(req_count, cand_count, HEADS, head_dim)).reshape(
        req_count, cand_count, model_width
    )
    average = jnp.mean(attended, axis=2, keepdims=True)
    variance = jnp.mean((attended - average) ** 2, axis=2, keepdims=True)
    gated = (
        (attended - average) / jnp.sqrt(variance + 1e-05) * norm_gain * gate_u.astype(jnp.float32)
    ).astype(jnp.bfloat16)
    gated_rows = gated.reshape(req_count * cand_count, model_width)
    branch = jnp.dot(gated_rows, out_weight, preferred_element_type=jnp.float32)
    branch = branch.reshape(req_count, cand_count, model_width)
    result = cand_embed.astype(jnp.float32) + is_live.astype(jnp.float32)[:, :, None] * branch
    return result.astype(jnp.bfloat16)


def solution(mesh):
    in_specs = (
        P("req", "hist", None),
        P("req", "hist", None),
        P("req", "hist", None),
        P("req", None),
        P(),
        P(),
        P("req"),
        P("req"),
        P("req", "hist", None),
    )
    out_specs = P("req", "hist", None)
    paired = mesh.shape["hist"] == 2 and mesh.shape["req"] == LINE * PLANE
    return jax.shard_map(
        on_device_kernel if paired else on_device,
        mesh=mesh, in_specs=in_specs, out_specs=out_specs, check_vma=False,
    )
```
